32 devices in a mesh: leaf: 8 (over z, y), sub: 4 (over x, core).
Axes of the slice: x: 2, y: 2, z: 4, core: 2. Of those that a mesh axis runs over, the one named last changes fastest.
Arguments:
- sources: bfloat16 [32, 262144], P(None, ('leaf', 'sub')), may hold values from -6 to 6
- leaf_basis: bfloat16 [2048, 64, 128], P(('leaf', 'sub')), may hold values from -0.5 to 0.5
- near_blocks: bfloat16 [6144, 128, 128], P(('leaf', 'sub')), may hold values from -0.3125 to 0.3125
- near_index: int32 [6144, 2], P(('leaf', 'sub')), may hold values from 0 to 2047, as said below
- near_count: int32 [32], P(('leaf', 'sub')), may hold values from 96 to 192, as said below
- transfer: bfloat16 [4064, 4096], P(('leaf', 'sub')), may hold values from -0.5 to 0.5
- couple_first: bfloat16 [6144, 4096], P(('leaf', 'sub')), may hold values from -0.4375 to 0.4375
- couple_second: bfloat16 [3072, 4096], P(('leaf', 'sub')), may hold values from -0.4375 to 0.4375
- couple_third: bfloat16 [1536, 4096], P(('leaf', 'sub')), may hold values from -0.4375 to 0.4375
- index_first: int32 [6144, 2], P(('leaf', 'sub')), may hold values from 0 to 2047, as said below
- index_second: int32 [3072, 2], P(('leaf', 'sub')), may hold values from 0 to 1023, as said below
- index_third: int32 [1536, 2], P(('leaf', 'sub')), may hold values from 0 to 511, as said below
- couple_count: int32 [32, 3], P(('leaf', 'sub')), may hold values from 24 to 192, as said below
- fold_transfer: bfloat16 [16, 4096], replicated, may hold values from -0.5 to 0.5
- top_couple: bfloat16 [8, 8, 4096], P('leaf'), may hold values from -0.75 to 0.75
Outputs:
- potential: float32 [32, 262144], P(None, ('leaf', 'sub'))
The draws below stay inside these ranges and needn't reach their ends.
Inputs may be any that keep to these rules, and one draw needn't show every extreme that they name: `near_index`: the slots of one device list each of its 64 leaves as row leaf 3 times, in the order of the leaves repeated; a slot's column leaf lies at most 16 leaves from its row leaf. Only the first near_count[d] slots of device d are live; some device has all its slots live. `index_first`: the slots of one device list each of its level-0 nodes as row node 3 times, in the order of the nodes repeated; a partner node lies 2 or 3 nodes from its row node. `index_second`: the slots of one device list each of its level-1 nodes as row node 3 times, in the order of the nodes repeated; a partner node lies 2 or 3 nodes from its row node. `index_third`: the slots of one device list each of its level-2 nodes as row node 3 times, in the order of the nodes repeated; a partner node lies 2 or 3 nodes from its row node. `couple_count`: column j counts the live slots of level j, at least half of them; at each level some device has all its slots live.
All inputs are finite; a program needn't handle non-finite values.
Results may differ from the reference program's by a relative error of at most 0.02.
Values may be sent and summed in bfloat16 or wider, within the bound.
A program may use at most 64 MiB of HBM per device.

```python
import jax
import jax.numpy as jnp
from jax import lax

LEAF = 128
RANK = 64
RHS = 32
LEAVES_DEV = 64
REACH = 16
NEAR_PER = 3
PARTNERS = 3
COUPLED = 3
NEAR_DEV = 192
LEAVES = 2048
POINTS = 262144
NEAR = 6144
SLOTS_ONE = 6144
SLOTS_TWO = 3072
SLOTS_THREE = 1536
TRANS = 4064
FOLD = 16
N_LEAF = 8
N_SUB = 4


def slot_pairs(node_count, slot_count, offsets, node_limit):
    devices = LEAVES // LEAVES_DEV
    position = jnp.arange(devices * slot_count, dtype=jnp.int32)
    row_nodes = position // slot_count * node_count + position % node_count
    target = row_nodes + offsets
    target = jnp.where((target < 0) | (target >= node_limit), row_nodes - offsets, target)
    return jnp.stack([row_nodes, target], axis=1).astype(jnp.int32)


def level_pairs(key, level_no):
    devices = LEAVES // LEAVES_DEV
    node_count = LEAVES_DEV // 2 ** level_no
    slot_count = PARTNERS * node_count
    offset_table = jnp.array([-3, -2, 2, 3], dtype=jnp.int32)
    chosen = offset_table[jax.random.randint(key, (devices * slot_count,), 0, 4)]
    return slot_pairs(node_count, slot_count, chosen, LEAVES // 2 ** level_no)


def spread_counts(key, most, devices):
    lowest = most // 2
    counts = jax.random.randint(key, (devices,), lowest, most + 1)
    shuffled = jax.random.permutation(jax.random.fold_in(key, 1), devices)
    counts = counts.at[shuffled[0]].set(most).at[shuffled[1]].set(lowest)
    return counts.astype(jnp.int32)


def draw_near_index(key, part):
    key = jax.random.fold_in(key, 11)
    offsets = jax.random.randint(key, (NEAR,), -REACH, REACH + 1)
    return slot_pairs(LEAVES_DEV, NEAR_DEV, offsets, LEAVES)


def draw_near_count(key, part):
    key = jax.random.fold_in(key, 12)
    return spread_counts(key, NEAR_DEV, LEAVES // LEAVES_DEV)


def draw_index_first(key, part):
    key = jax.random.fold_in(key, 13)
    return level_pairs(key, 0)


def draw_index_second(key, part):
    key = jax.random.fold_in(key, 14)
    return level_pairs(key, 1)


def draw_index_third(key, part):
    key = jax.random.fold_in(key, 15)
    return level_pairs(key, 2)


def draw_couple_count(key, part):
    key = jax.random.fold_in(key, 16)
    devices = LEAVES // LEAVES_DEV
    columns = []
    for level_no in range(COUPLED):
        columns.append(spread_counts(jax.random.fold_in(key, 100 + level_no), PARTNERS * (LEAVES_DEV // 2 ** level_no), devices))
    return jnp.stack(columns, axis=1).astype(jnp.int32)


def block_scale(key, dims, shards, least, top_value):
    def one(dim, shards_of):
        heights = jax.random.uniform(jax.random.fold_in(jax.random.fold_in(key, 6), dim), (shards_of,), jnp.float32, least / len(shards), top_value / len(shards))
        return jnp.repeat(jnp.exp(heights), dims[dim] // shards_of).reshape((-1,) + (1,) * (len(dims) - dim - 1))

    gain = one(*shards[0])
    for cut in shards[1:]:
        gain = gain * one(*cut)
    return gain


def centred(own_key, shape, deviation, reach, shards=(), kind=jnp.bfloat16):
    gain = block_scale(own_key, shape, shards, -0.22, 0.18) if shards else 1.0
    result = jax.random.normal(own_key, shape, jnp.float32) * deviation * gain
    return jnp.minimum(jnp.maximum(result, -reach), reach).astype(kind)


def setup_inputs(seed: int = 0) -> dict:
    streams_of = jax.random.split(jax.random.key(seed), 16)
    sources = centred(streams_of[0], (RHS, POINTS), 1.0, 6.0, ((1, 32),))
    leaf_basis = centred(streams_of[1], (LEAVES, RANK, LEAF), LEAF ** -0.5, 0.5, ((0, 32),))
    near_blocks = centred(streams_of[2], (NEAR, LEAF, LEAF), (LEAF * NEAR_PER) ** -0.5, 0.3125, ((0, 32),))
    near_index = draw_near_index(jax.random.fold_in(streams_of[15], 71), 0)
    near_count = draw_near_count(jax.random.fold_in(streams_of[15], 71), 0)
    transfer = centred(streams_of[5], (TRANS, RANK * RANK), (2 * RANK) ** -0.5, 0.5, ((0, 32),))
    couple_first = centred(streams_of[6], (SLOTS_ONE, RANK * RANK), (PARTNERS * RANK) ** -0.5, 0.4375, ((0, 32),))
    couple_second = centred(streams_of[7], (SLOTS_TWO, RANK * RANK), (PARTNERS * RANK) ** -0.5, 0.4375, ((0, 32),))
    couple_third = centred(streams_of[8], (SLOTS_THREE, RANK * RANK), (PARTNERS * RANK) ** -0.5, 0.4375, ((0, 32),))
    index_first = draw_index_first(jax.random.fold_in(streams_of[15], 71), 0)
    index_second = draw_index_second(jax.random.fold_in(streams_of[15], 71), 0)
    index_third = draw_index_third(jax.random.fold_in(streams_of[15], 71), 0)
    couple_count = draw_couple_count(jax.random.fold_in(streams_of[15], 71), 0)
    fold_transfer = centred(streams_of[13], (FOLD, RANK * RANK), (2 * RANK) ** -0.5, 0.5)
    top_couple = centred(streams_of[14], (N_LEAF, N_LEAF, RANK * RANK), RANK ** -0.5, 0.75, ((0, 8),))
    return dict(sources=sources, leaf_basis=leaf_basis, near_blocks=near_blocks, near_index=near_index, near_count=near_count, transfer=transfer, couple_first=couple_first, couple_second=couple_second, couple_third=couple_third, index_first=index_first, index_second=index_second, index_third=index_third, couple_count=couple_count, fold_transfer=fold_transfer, top_couple=top_couple)


highest = lax.Precision.HIGHEST


def as_float(array):
    return array.astype(jnp.float32)


def fold_upward(terms, fold_mats):
    columns, groups, members, rank_size = terms.shape
    current = terms.reshape(columns, groups, members // 2, 2, rank_size).sum(3).astype(jnp.bfloat16)
    kept_levels = [current]
    offset = 0
    members = members // 2
    while members > 1:
        matrices = fold_mats[:, offset:offset + members]
        products = jnp.einsum("rgnk,gnkm->rgnm", as_float(current), as_float(matrices), precision=highest)
        offset = offset + members
        current = products.reshape(columns, groups, members // 2, 2, rank_size).sum(3).astype(jnp.bfloat16)
        kept_levels.append(current)
        members = members // 2
    return kept_levels


def fold_downward(top_field, fold_mats, members):
    current = top_field
    node_count = 2
    while node_count <= members // 2:
        matrices = fold_mats[:, members - 2 * node_count:members - node_count]
        expanded = jnp.repeat(current.astype(jnp.bfloat16), 2, axis=2)
        current = jnp.einsum("rgnm,gnkm->rgnk", as_float(expanded), as_float(matrices), precision=highest)
        node_count = node_count * 2
    return current


def couple_global(coefficients, matrices, indices, live_counts, node_count):
    devices = live_counts.shape[0]
    slot_count = matrices.shape[0] // devices
    rank_size = coefficients.shape[2]
    mats_dev = matrices.reshape(devices, slot_count, rank_size, rank_size)
    index_dev = indices.reshape(devices, slot_count, 2)

    def couple_part(inputs):
        blocks, slot_index, live_count, device = inputs
        picked = as_float(jnp.take(coefficients, slot_index[:, 1], axis=1))
        products = jnp.einsum("rsk,skm->rsm", picked, as_float(blocks), precision=highest)
        live_mask = jnp.arange(slot_count, dtype=jnp.int32) < live_count
        local_rows = slot_index[:, 0] - device * node_count
        onehot = jnp.where((local_rows[:, None] == jnp.arange(node_count, dtype=jnp.int32)[None, :]) & live_mask[:, None], 1.0, 0.0).astype(jnp.float32)
        return jnp.einsum("rsm,sn->rnm", products, onehot, precision=highest)

    device_parts = lax.map(couple_part, (mats_dev, index_dev, live_counts, jnp.arange(devices, dtype=jnp.int32)))
    return device_parts.transpose(1, 0, 2, 3).reshape(coefficients.shape[0], devices * node_count, rank_size)


def reference(sources, leaf_basis, near_blocks, near_index, near_count, transfer, couple_first, couple_second, couple_third, index_first, index_second, index_third, couple_count, fold_transfer, top_couple):
    devices = N_LEAF * N_SUB
    source_leaves = sources.reshape(RHS, LEAVES, LEAF)
    blocks_dev = near_blocks.reshape(devices, NEAR_DEV, LEAF, LEAF)
    index_dev = near_index.reshape(devices, NEAR_DEV, 2)

    def near_part(inputs):
        blocks, slot_index, live_count, device = inputs
        picked = as_float(jnp.take(source_leaves, slot_index[:, 1], axis=1))
        products = jnp.einsum("bij,rbj->rbi", as_float(blocks), picked, precision=highest)
        live_mask = jnp.arange(NEAR_DEV, dtype=jnp.int32) < live_count
        local_rows = slot_index[:, 0] - device * LEAVES_DEV
        onehot = jnp.where((local_rows[:, None] == jnp.arange(LEAVES_DEV, dtype=jnp.int32)[None, :]) & live_mask[:, None], 1.0, 0.0).astype(jnp.float32)
        return jnp.einsum("rbi,bl->rli", products, onehot, precision=highest)

    near_parts = lax.map(near_part, (blocks_dev, index_dev, near_count, jnp.arange(devices, dtype=jnp.int32)))
    near_field = near_parts.transpose(1, 0, 2, 3).reshape(RHS, LEAVES, LEAF)

    tree_depth = LEAVES_DEV.bit_length() - 1
    transfer_dev = transfer.reshape(devices, 2 * LEAVES_DEV - 1, RANK, RANK)

    def level_mats(level_no):
        node_count = LEAVES_DEV >> level_no
        start_row = 2 * LEAVES_DEV - 2 * node_count
        return transfer_dev[:, start_row:start_row + node_count].reshape(devices * node_count, RANK, RANK)

    coefficient = jnp.einsum("lkp,rlp->rlk", as_float(leaf_basis), as_float(source_leaves), precision=highest).astype(jnp.bfloat16)
    levels = [coefficient]
    for level_no in range(tree_depth):
        products = jnp.einsum("rnk,nkm->rnm", as_float(levels[level_no]), as_float(level_mats(level_no)), precision=highest)
        levels.append(products.reshape(RHS, -1, 2, RANK).sum(2).astype(jnp.bfloat16))
    top_terms = jnp.einsum("rnk,nkm->rnm", as_float(levels[tree_depth]), as_float(level_mats(tree_depth)), precision=highest)

    couples = ((couple_first, index_first), (couple_second, index_second), (couple_third, index_third))
    fields = []
    for level_no in range(COUPLED):
        fields.append(couple_global(levels[level_no], couples[level_no][0], couples[level_no][1], couple_count[:, level_no], LEAVES_DEV >> level_no))

    fold_mats = fold_transfer.reshape(N_LEAF, N_SUB - 2, RANK, RANK)
    kept_levels = fold_upward(top_terms.reshape(RHS, N_LEAF, N_SUB, RANK), fold_mats)
    top_coeffs = kept_levels[-1][:, :, 0, :]
    top_mats = top_couple.reshape(N_LEAF, N_LEAF, RANK, RANK)
    node_ids = jnp.arange(N_LEAF, dtype=jnp.int32)
    far_mask = jnp.where(jnp.abs(node_ids[:, None] - node_ids[None, :]) >= 2, 1.0, 0.0).astype(jnp.float32)
    top_products = jnp.einsum("rjk,ijkm->rijm", as_float(top_coeffs), as_float(top_mats), precision=highest)
    top_field = jnp.einsum("rijm,ij->rim", top_products, far_mask, precision=highest)

    down_field = fold_downward(top_field[:, :, None, :], fold_mats, N_SUB)
    down_field = down_field.reshape(RHS, N_LEAF * (N_SUB // 2), RANK)
    expanded = jnp.repeat(down_field.astype(jnp.bfloat16), 2, axis=1)
    down_field = jnp.einsum("rnm,nkm->rnk", as_float(expanded), as_float(level_mats(tree_depth)), precision=highest)
    for level_no in reversed(range(tree_depth)):
        expanded = jnp.repeat(down_field.astype(jnp.bfloat16), 2, axis=1)
        down_field = jnp.einsum("rnm,nkm->rnk", as_float(expanded), as_float(level_mats(level_no)), precision=highest)
        if level_no < COUPLED:
            down_field = down_field + fields[level_no]
    far_field = jnp.einsum("rlk,lkp->rlp", as_float(down_field.astype(jnp.bfloat16)), as_float(leaf_basis), precision=highest)
    return (near_field + far_field).reshape(RHS, POINTS)
```

```python
import functools

import jax
import jax.numpy as jnp
from jax import lax
from jax.experimental import pallas as pl
from jax.experimental.pallas import tpu as pltpu
from jax.sharding import PartitionSpec as P

REACH = 16
COUPLED = 3
HALO = 3
CHUNKS = 4
MESH = pl.DeviceIdType.MESH
BF = jnp.bfloat16
F32 = jnp.float32


def dot_nn(a, b):
    return lax.dot_general(a, b, (((1,), (0,)), ((), ())), preferred_element_type=F32)


def dot_nt(a, b):
    return lax.dot_general(a, b, (((1,), (1,)), ((), ())), preferred_element_type=F32)


def spread(rank):
    row = lax.broadcasted_iota(jnp.int32, (2 * rank, 2 * rank), 0)
    col = lax.broadcasted_iota(jnp.int32, (2 * rank, 2 * rank), 1)
    inner = row % rank
    place = (row // rank) * rank + (inner % 2) * (rank // 2) + inner // 2
    return jnp.where(place == col, 1.0, 0.0).astype(BF)


def kernel(
    dims,
    idx,
    sources,
    basis,
    near,
    transfer,
    first,
    second,
    third,
    fold,
    top,
    out,
    xs,
    xl,
    vb,
    vn,
    vt,
    v1,
    v2,
    v3,
    vf,
    vtop,
    ft,
    f1,
    f2,
    f3,
    ff,
    ftop,
    wt,
    cp0,
    cp1,
    cp2,
    chi,
    g0,
    g1,
    g2,
    dn,
    terms,
    tc,
    load_sem,
    near_sem,
    halo_send,
    halo_recv,
    coef_send,
    coef_recv,
    sub_send,
    sub_recv,
    leaf_send,
    leaf_recv,
):
    groups, members, leaves, columns, rank, points = dims
    depth = leaves.bit_length() - 1
    lf = lax.axis_index("leaf")
    sb = lax.axis_index("sub")
    me = lf * members + sb
    count = groups * members
    right = lax.rem(me + 1, count)
    left = lax.rem(me + count - 1, count)
    right_id = (right // members, lax.rem(right, members))
    left_id = (left // members, lax.rem(left, members))
    half = rank // 2
    wide = REACH * points
    own = leaves * points

    loads = []
    pairs = (
        (transfer, vt),
        (sources, xs.at[:, pl.ds(wide, own)]),
        (basis, vb),
        (fold, vf),
        (top, vtop),
        (first, v1),
        (second, v2),
        (third, v3),
    )
    for i, (src, dst) in enumerate(pairs):
        copy = pltpu.make_async_copy(src, dst, load_sem.at[i])
        copy.start()
        loads.append(copy)
    part = leaves // CHUNKS
    near_loads = []
    for i in range(CHUNKS):
        copy = pltpu.make_async_copy(
            near.at[:, pl.ds(i * part, part)], vn.at[:, pl.ds(i * part, part)], near_sem.at[i]
        )
        copy.start()
        near_loads.append(copy)

    sub_ids = [(lf, lax.rem(sb + k, members)) for k in range(1, members)]
    leaf_ids = [(lax.rem(lf + k, groups), sb) for k in range(1, groups)]
    everyone = [left_id, right_id] + sub_ids + leaf_ids
    barrier = pltpu.get_barrier_semaphore()
    for target in everyone:
        pl.semaphore_signal(barrier, inc=1, device_id=target, device_id_type=MESH)

    perm = spread(rank)
    small = perm[:rank, :rank]

    def relay(src, dst):
        rows = src.shape[0]
        step = 8

        def body(q, carry):
            vals = []
            for u in range(step):
                p = q * step + u
                block = src[:, pl.ds(pl.multiple_of(p * 2 * rank, 2 * rank), 2 * rank)]
                vals.append(dot_nn(block, perm))
            for u in range(step):
                dst[pl.ds(q * step + u, rows, stride=half), :] = vals[u]
            return carry

        lax.fori_loop(0, half // step, body, 0)

    def matrix(ref, s):
        m = ref[pl.ds(pl.multiple_of(s * half, half), half), :].astype(BF)
        return jnp.concatenate([m[:, :rank], m[:, rank:]], axis=0)

    def blocks(n, width, compute, store):
        width = min(width, n)

        def body(q, carry):
            vals = [compute(q * width + u) for u in range(width)]
            for u in range(width):
                store(q * width + u, vals[u])
            return carry

        if n == width:
            body(0, 0)
        else:
            lax.fori_loop(0, n // width, body, 0)

    loads[0].wait()
    relay(vt, ft)

    def put_wt(s, value):
        wt[s] = value

    for start in range(2 * leaves - 1 - (2 * leaves - 1) % 8, 2 * leaves - 1):
        wt[start] = matrix(ft, start)
    blocks((2 * leaves - 1) // 8 * 8, 8, functools.partial(matrix, ft), put_wt)

    pl.semaphore_wait(barrier, len(everyone))
    halo = [
        pltpu.make_async_remote_copy(
            src_ref=sources.at[:, pl.ds(own - wide, wide)],
            dst_ref=xs.at[:, pl.ds(0, wide)],
            send_sem=halo_send.at[0],
            recv_sem=halo_recv.at[0],
            device_id=right_id,
            device_id_type=MESH,
        ),
        pltpu.make_async_remote_copy(
            src_ref=sources.at[:, pl.ds(0, wide)],
            dst_ref=xs.at[:, pl.ds(wide + own, wide)],
            send_sem=halo_send.at[1],
            recv_sem=halo_recv.at[1],
            device_id=left_id,
            device_id_type=MESH,
        ),
    ]
    for copy in halo:
        copy.start()

    every = leaves + 2 * REACH
    xl[every] = jnp.zeros((columns, points), BF)
    coefs = (cp0, cp1, cp2)
    for j, ref in enumerate(coefs):
        ref[(leaves >> j) + 2 * HALO] = jnp.zeros((columns, rank), BF)

    loads[1].wait()
    loads[2].wait()

    def leaf_body(q, carry):
        vals = []
        for u in range(8):
            leaf = q * 8 + u
            x = xs[:, pl.ds(pl.multiple_of(wide + leaf * points, points), points)]
            vals.append(dot_nt(x, vb[leaf]).astype(BF))
        mixed = dot_nn(jnp.concatenate(vals, axis=0), small).astype(BF)
        for u in range(8):
            cp0[HALO + q * 8 + u] = mixed[u * columns : (u + 1) * columns]
        return carry

    lax.fori_loop(0, leaves // 8, leaf_body, 0)

    high_start = {}
    position = 0
    for j in range(COUPLED, depth + 1):
        high_start[j] = position
        position += leaves >> j

    def place(j):
        return (coefs[j], HALO) if j < COUPLED else (chi, high_start[j])

    for j in range(depth):
        src, src_at = place(j)
        dst, dst_at = place(j + 1)
        row = 2 * leaves - 2 * (leaves >> j)

        def up(n, src=src, src_at=src_at, row=row):
            a = dot_nn(src[src_at + 2 * n], wt[row + 2 * n])
            b = dot_nn(src[src_at + 2 * n + 1], wt[row + 2 * n + 1])
            return (a + b).astype(BF)

        def put(n, value, dst=dst, dst_at=dst_at):
            dst[dst_at + n] = value

        blocks(leaves >> (j + 1), 8, up, put)

    root = 2 * leaves - 2
    terms[sb] = dot_nn(chi[high_start[depth]], wt[root])
    sub_copies = [
        pltpu.make_async_remote_copy(
            src_ref=terms.at[sb],
            dst_ref=terms.at[sb],
            send_sem=sub_send.at[k],
            recv_sem=sub_recv.at[k],
            device_id=target,
            device_id_type=MESH,
        )
        for k, target in enumerate(sub_ids)
    ]
    for copy in sub_copies:
        copy.start()
    coef_copies = []
    for j, ref in enumerate(coefs):
        n = leaves >> j
        for side, (src_at, dst_at, target) in enumerate(
            ((n, 0, right_id), (HALO, n + HALO, left_id))
        ):
            copy = pltpu.make_async_remote_copy(
                src_ref=ref.at[pl.ds(src_at, HALO)],
                dst_ref=ref.at[pl.ds(dst_at, HALO)],
                send_sem=coef_send.at[2 * j + side],
                recv_sem=coef_recv.at[2 * j + side],
                device_id=target,
                device_id_type=MESH,
            )
            copy.start()
            coef_copies.append(copy)

    loads[3].wait()
    relay(vf, ff)
    loads[4].wait()
    relay(vtop, ftop)

    for copy in sub_copies:
        copy.wait()
    fold_row = lf * (members - 2)
    current = [(terms[2 * n] + terms[2 * n + 1]).astype(BF) for n in range(members // 2)]
    offset = 0
    while len(current) > 1:
        products = [
            dot_nn(c, matrix(ff, fold_row + offset + n)) for n, c in enumerate(current)
        ]
        offset += len(current)
        current = [
            (products[2 * n] + products[2 * n + 1]).astype(BF)
            for n in range(len(products) // 2)
        ]
    tc[lf] = current[0]
    leaf_copies = [
        pltpu.make_async_remote_copy(
            src_ref=tc.at[lf],
            dst_ref=tc.at[lf],
            send_sem=leaf_send.at[k],
            recv_sem=leaf_recv.at[k],
            device_id=target,
            device_id_type=MESH,
        )
        for k, target in enumerate(leaf_ids)
    ]
    for copy in leaf_copies:
        copy.start()

    loads[5].wait()
    relay(v1, f1)
    loads[6].wait()
    relay(v2, f2)
    loads[7].wait()
    relay(v3, f3)
    for copy in coef_copies:
        copy.wait()
    base = 3 * leaves
    for j, (mats, field) in enumerate(((f1, g0), (f2, g1), (f3, g2))):
        n = leaves >> j
        ref = coefs[j]

        def couple(i, n=n, ref=ref, mats=mats, base=base):
            total = None
            for t in range(3):
                s = t * n + i
                value = dot_nn(ref[idx[base + s]], matrix(mats, s))
                total = value if total is None else total + value
            return total

        def put_field(i, value, field=field):
            field[i] = value

        blocks(n, 8, couple, put_field)
        base += 3 * n

    for copy in halo:
        copy.wait()
    for copy in near_loads:
        copy.wait()

    def load_leaf(leaf):
        return xs[:, pl.ds(pl.multiple_of(leaf * points, points), points)]

    def put_leaf(leaf, value):
        xl[leaf] = value

    blocks(every, 8, load_leaf, put_leaf)

    def near_leaf(leaf):
        total = None
        for t in range(3):
            value = dot_nt(xl[idx[t * leaves + leaf]], vn[t, leaf])
            total = value if total is None else total + value
        return total

    def put_near(leaf, value):
        out[:, pl.ds(pl.multiple_of(leaf * points, points), points)] = value

    blocks(leaves, 8, near_leaf, put_near)

    for copy in leaf_copies:
        copy.wait()
    down = jnp.zeros((columns, rank), F32)
    for t in range(groups):
        far = jnp.where(jnp.abs(lf - t) >= 2, 1.0, 0.0).astype(F32)
        down = down + far * dot_nn(tc[t], matrix(ftop, t))
    nodes = 2
    while nodes <= members // 2:
        row = fold_row + members - 2 * nodes + sb * nodes // members
        down = dot_nt(down.astype(BF), matrix(ff, row))
        nodes *= 2
    down = dot_nt(down.astype(BF), wt[root])
    down_start = {depth: 0}
    position = 1
    for j in reversed(range(depth)):
        down_start[j] = position
        position += leaves >> j
    dn[0] = down.astype(BF)
    fields = (g0, g1, g2)
    for j in reversed(range(depth)):
        row = 2 * leaves - 2 * (leaves >> j)
        src_at, dst_at = down_start[j + 1], down_start[j]

        def descend(c, row=row, src_at=src_at, j=j):
            value = dot_nt(dn[src_at + c // 2], wt[row + c])
            if j < COUPLED:
                value = value + fields[j][c]
            return value.astype(BF)

        def put_down(c, value, dst_at=dst_at):
            dn[dst_at + c] = value

        blocks(leaves >> j, 8, descend, put_down)

    def final_body(q, carry):
        rows = jnp.concatenate([dn[down_start[0] + q * 8 + u] for u in range(8)], axis=0)
        natural = dot_nt(rows, small).astype(BF)
        for u in range(8):
            leaf = q * 8 + u
            at = pl.ds(pl.multiple_of(leaf * points, points), points)
            out[:, at] = out[:, at] + dot_nn(
                natural[u * columns : (u + 1) * columns], vb[leaf]
            )
        return carry

    lax.fori_loop(0, leaves // 8, final_body, 0)


def local(
    sources,
    leaf_basis,
    near_blocks,
    near_index,
    near_count,
    transfer,
    couple_first,
    couple_second,
    couple_third,
    index_first,
    index_second,
    index_third,
    couple_count,
    fold_transfer,
    top_couple,
):
    columns = sources.shape[0]
    leaves, rank, points = leaf_basis.shape
    groups = lax.axis_size("leaf")
    members = lax.axis_size("sub")
    device = lax.axis_index(("leaf", "sub"))

    def slots(index, live, first_node, dead):
        n = index.shape[0]
        return jnp.where(lax.iota(jnp.int32, n) < live, index[:, 1] - first_node, dead)

    lists = [slots(near_index, near_count[0], device * leaves - REACH, leaves + 2 * REACH)]
    for j, index in enumerate((index_first, index_second, index_third)):
        n = leaves >> j
        lists.append(slots(index, couple_count[0, j], device * n - HALO, n + 2 * HALO))
    idx = jnp.concatenate(lists)

    near = near_blocks.reshape(3, leaves, points, points)
    top = top_couple.reshape(groups, rank * rank)
    trans = transfer.shape[0]
    half = rank // 2

    def flat(n):
        return pltpu.VMEM((n * half, 2 * rank), F32)

    scratch = [
        pltpu.VMEM((columns, (leaves + 2 * REACH) * points), BF),
        pltpu.VMEM((leaves + 2 * REACH + 1, columns, points), BF),
        pltpu.VMEM(leaf_basis.shape, BF),
        pltpu.VMEM(near.shape, BF),
        pltpu.VMEM(transfer.shape, BF),
        pltpu.VMEM(couple_first.shape, BF),
        pltpu.VMEM(couple_second.shape, BF),
        pltpu.VMEM(couple_third.shape, BF),
        pltpu.VMEM(fold_transfer.shape, BF),
        pltpu.VMEM(top.shape, BF),
        flat(trans),
        flat(couple_first.shape[0]),
        flat(couple_second.shape[0]),
        flat(couple_third.shape[0]),
        flat(fold_transfer.shape[0]),
        flat(groups),
        pltpu.VMEM((trans, rank, rank), BF),
    ]
    for j in range(COUPLED):
        scratch.append(pltpu.VMEM(((leaves >> j) + 2 * HALO + 1, columns, rank), BF))
    scratch.append(pltpu.VMEM(((leaves >> (COUPLED - 1)) - 1, columns, rank), BF))
    for j in range(COUPLED):
        scratch.append(pltpu.VMEM((leaves >> j, columns, rank), F32))
    scratch.append(pltpu.VMEM((2 * leaves - 1, columns, rank), BF))
    scratch.append(pltpu.VMEM((members, columns, rank), F32))
    scratch.append(pltpu.VMEM((groups, columns, rank), BF))
    for n in (8, CHUNKS, 2, 2, 6, 6, members - 1, members - 1, groups - 1, groups - 1):
        scratch.append(pltpu.SemaphoreType.DMA((n,)))

    anywhere = pl.BlockSpec(memory_space=pl.ANY)
    dims = (groups, members, leaves, columns, rank, points)
    return pl.pallas_call(
        functools.partial(kernel, dims),
        out_shape=jax.ShapeDtypeStruct((columns, leaves * points), F32),
        in_specs=[pl.BlockSpec(memory_space=pltpu.SMEM)] + [anywhere] * 9,
        out_specs=pl.BlockSpec(memory_space=pltpu.VMEM),
        scratch_shapes=scratch,
        compiler_params=pltpu.CompilerParams(
            collective_id=0, has_side_effects=True, vmem_limit_bytes=56 * 1024 * 1024
        ),
        cost_estimate=pl.CostEstimate(
            flops=600_000_000, bytes_accessed=13_000_000, transcendentals=0
        ),
        name="operator",
    )(
        idx,
        sources,
        leaf_basis,
        near,
        transfer,
        couple_first,
        couple_second,
        couple_third,
        fold_transfer,
        top,
    )


def solution(mesh):
    both = ("leaf", "sub")
    return jax.shard_map(
        local,
        mesh=mesh,
        in_specs=(
            P(None, both),
            P(both, None, None),
            P(both, None, None),
            P(both, None),
            P(both),
            P(both, None),
            P(both, None),
            P(both, None),
            P(both, None),
            P(both, None),
            P(both, None),
            P(both, None),
            P(both, None),
            P(),
            P("leaf", None, None),
        ),
        out_specs=P(None, both),
        check_vma=False,
    )
```

```python
import functools

import jax
import jax.numpy as jnp
from jax import lax
from jax.experimental import pallas as pl
from jax.experimental.pallas import tpu as pltpu
from jax.sharding import PartitionSpec as P

REACH = 16
COUPLED = 3
HALO = 3
CHUNKS = 4
MESH = pl.DeviceIdType.MESH
BF = jnp.bfloat16
F32 = jnp.float32


def dot_nn(a, b):
    return lax.dot_general(a, b, (((1,), (0,)), ((), ())), preferred_element_type=F32)


def dot_nt(a, b):
    return lax.dot_general(a, b, (((1,), (1,)), ((), ())), preferred_element_type=F32)


def spread(rank):
    row = lax.broadcasted_iota(jnp.int32, (2 * rank, 2 * rank), 0)
    col = lax.broadcasted_iota(jnp.int32, (2 * rank, 2 * rank), 1)
    inner = row % rank
    place = (row // rank) * rank + (inner % 2) * (rank // 2) + inner // 2
    return jnp.where(place == col, 1.0, 0.0).astype(BF)


def kernel(
    dims,
    near_at,
    first_at,
    second_at,
    third_at,
    near_live,
    couple_live,
    sources,
    basis,
    near,
    transfer,
    first,
    second,
    third,
    fold,
    top,
    out,
    xs,
    xl,
    vb,
    vn,
    vt,
    v1,
    v2,
    v3,
    vf,
    vtop,
    ft,
    f1,
    f2,
    f3,
    ff,
    ftop,
    wt,
    cp0,
    cp1,
    cp2,
    chi,
    g0,
    g1,
    g2,
    dn,
    terms,
    tc,
    load_sem,
    near_sem,
    halo_send,
    halo_recv,
    coef_send,
    coef_recv,
    sub_send,
    sub_recv,
    leaf_send,
    leaf_recv,
):
    groups, members, leaves, columns, rank, points = dims
    depth = leaves.bit_length() - 1
    lf = lax.axis_index("leaf")
    sb = lax.axis_index("sub")
    me = lf * members + sb
    count = groups * members
    right = lax.rem(me + 1, count)
    left = lax.rem(me + count - 1, count)
    right_id = (right // members, lax.rem(right, members))
    left_id = (left // members, lax.rem(left, members))
    half = rank // 2
    wide = REACH * points
    own = leaves * points

    loads = []
    pairs = (
        (sources, xs.at[:, pl.ds(wide, own)]),
        (basis, vb),
        (transfer, vt),
        (fold, vf),
        (top, vtop),
        (first, v1),
        (second, v2),
        (third, v3),
    )
    for i, (src, dst) in enumerate(pairs):
        copy = pltpu.make_async_copy(src, dst, load_sem.at[i])
        copy.start()
        loads.append(copy)
    part = leaves // CHUNKS
    near_loads = []
    for i in range(CHUNKS):
        copy = pltpu.make_async_copy(
            near.at[:, pl.ds(i * part, part)], vn.at[:, pl.ds(i * part, part)], near_sem.at[i]
        )
        copy.start()
        near_loads.append(copy)

    sub_ids = [(lf, lax.rem(sb + k, members)) for k in range(1, members)]
    leaf_ids = [(lax.rem(lf + k, groups), sb) for k in range(1, groups)]
    everyone = [left_id, right_id] + sub_ids + leaf_ids
    barrier = pltpu.get_barrier_semaphore()
    for target in everyone:
        pl.semaphore_signal(barrier, inc=1, device_id=target, device_id_type=MESH)

    perm = spread(rank)
    small = perm[:rank, :rank]

    def relay(src, dst):
        rows = src.shape[0]
        step = 8

        def body(q, carry):
            vals = []
            for u in range(step):
                p = q * step + u
                block = src[:, pl.ds(pl.multiple_of(p * 2 * rank, 2 * rank), 2 * rank)]
                vals.append(dot_nn(block, perm))
            for u in range(step):
                dst[pl.ds(q * step + u, rows, stride=half), :] = vals[u]
            return carry

        lax.fori_loop(0, half // step, body, 0)

    def matrix(ref, s):
        m = ref[pl.ds(pl.multiple_of(s * half, half), half), :].astype(BF)
        return jnp.concatenate([m[:, :rank], m[:, rank:]], axis=0)

    def blocks(n, width, compute, store):
        width = min(width, n)

        def body(q, carry):
            vals = [compute(q * width + u) for u in range(width)]
            for u in range(width):
                store(q * width + u, vals[u])
            return carry

        if n == width:
            body(0, 0)
        else:
            lax.fori_loop(0, n // width, body, 0)

    every = leaves + 2 * REACH
    xl[every] = jnp.zeros((columns, points), BF)
    coefs = (cp0, cp1, cp2)
    for j, ref in enumerate(coefs):
        ref[(leaves >> j) + 2 * HALO] = jnp.zeros((columns, rank), BF)

    loads[0].wait()
    loads[1].wait()

    def leaf_body(q, carry):
        vals = []
        for u in range(8):
            leaf = q * 8 + u
            x = xs[:, pl.ds(pl.multiple_of(wide + leaf * points, points), points)]
            vals.append(dot_nt(x, vb[leaf]).astype(BF))
        mixed = dot_nn(jnp.concatenate(vals, axis=0), small).astype(BF)
        for u in range(8):
            cp0[HALO + q * 8 + u] = mixed[u * columns : (u + 1) * columns]
        return carry

    lax.fori_loop(0, leaves // 8, leaf_body, 0)

    loads[2].wait()
    relay(vt, ft)

    def put_wt(s, value):
        wt[s] = value

    for start in range(2 * leaves - 1 - (2 * leaves - 1) % 8, 2 * leaves - 1):
        wt[start] = matrix(ft, start)
    blocks((2 * leaves - 1) // 8 * 8, 8, functools.partial(matrix, ft), put_wt)

    pl.semaphore_wait(barrier, len(everyone))
    halo = [
        pltpu.make_async_remote_copy(
            src_ref=sources.at[:, pl.ds(own - wide, wide)],
            dst_ref=xs.at[:, pl.ds(0, wide)],
            send_sem=halo_send.at[0],
            recv_sem=halo_recv.at[0],
            device_id=right_id,
            device_id_type=MESH,
        ),
        pltpu.make_async_remote_copy(
            src_ref=sources.at[:, pl.ds(0, wide)],
            dst_ref=xs.at[:, pl.ds(wide + own, wide)],
            send_sem=halo_send.at[1],
            recv_sem=halo_recv.at[1],
            device_id=left_id,
            device_id_type=MESH,
        ),
    ]
    for copy in halo:
        copy.start()

    high_start = {}
    position = 0
    for j in range(COUPLED, depth + 1):
        high_start[j] = position
        position += leaves >> j

    def place(j):
        return (coefs[j], HALO) if j < COUPLED else (chi, high_start[j])

    for j in range(depth):
        src, src_at = place(j)
        dst, dst_at = place(j + 1)
        row = 2 * leaves - 2 * (leaves >> j)

        def up(n, src=src, src_at=src_at, row=row):
            pair = jnp.concatenate([src[src_at + 2 * n], src[src_at + 2 * n + 1]], axis=1)
            both = wt[pl.ds(row + 2 * n, 2)].reshape(2 * rank, rank)
            return dot_nn(pair, both).astype(BF)

        def put(n, value, dst=dst, dst_at=dst_at):
            dst[dst_at + n] = value

        blocks(leaves >> (j + 1), 8, up, put)

    root = 2 * leaves - 2
    terms[sb] = dot_nn(chi[high_start[depth]], wt[root])
    sub_copies = [
        pltpu.make_async_remote_copy(
            src_ref=terms.at[sb],
            dst_ref=terms.at[sb],
            send_sem=sub_send.at[k],
            recv_sem=sub_recv.at[k],
            device_id=target,
            device_id_type=MESH,
        )
        for k, target in enumerate(sub_ids)
    ]
    for copy in sub_copies:
        copy.start()
    coef_copies = []
    for j, ref in enumerate(coefs):
        n = leaves >> j
        for side, (src_at, dst_at, target) in enumerate(
            ((n, 0, right_id), (HALO, n + HALO, left_id))
        ):
            copy = pltpu.make_async_remote_copy(
                src_ref=ref.at[pl.ds(src_at, HALO)],
                dst_ref=ref.at[pl.ds(dst_at, HALO)],
                send_sem=coef_send.at[2 * j + side],
                recv_sem=coef_recv.at[2 * j + side],
                device_id=target,
                device_id_type=MESH,
            )
            copy.start()
            coef_copies.append(copy)

    loads[3].wait()
    relay(vf, ff)
    loads[4].wait()
    relay(vtop, ftop)
    loads[5].wait()
    relay(v1, f1)
    loads[6].wait()
    relay(v2, f2)
    loads[7].wait()
    relay(v3, f3)

    for copy in sub_copies:
        copy.wait()
    fold_row = lf * (members - 2)
    current = [(terms[2 * n] + terms[2 * n + 1]).astype(BF) for n in range(members // 2)]
    offset = 0
    while len(current) > 1:
        products = [
            dot_nn(c, matrix(ff, fold_row + offset + n)) for n, c in enumerate(current)
        ]
        offset += len(current)
        current = [
            (products[2 * n] + products[2 * n + 1]).astype(BF)
            for n in range(len(products) // 2)
        ]
    tc[lf] = current[0]
    leaf_copies = [
        pltpu.make_async_remote_copy(
            src_ref=tc.at[lf],
            dst_ref=tc.at[lf],
            send_sem=leaf_send.at[k],
            recv_sem=leaf_recv.at[k],
            device_id=target,
            device_id_type=MESH,
        )
        for k, target in enumerate(leaf_ids)
    ]
    for copy in leaf_copies:
        copy.start()

    for copy in coef_copies:
        copy.wait()
    levels = ((f1, g0, first_at), (f2, g1, second_at), (f3, g2, third_at))
    for j, (mats, field, at) in enumerate(levels):
        n = leaves >> j
        ref = coefs[j]

        live = couple_live[0, j]

        def couple(i, n=n, ref=ref, mats=mats, at=at, live=live):
            rows, cols = [], []
            for t in range(3):
                s = t * n + i
                node = jnp.where(s < live, at[1, s] - (me * n - HALO), n + 2 * HALO)
                rows.append(ref[node])
                cols.append(matrix(mats, s))
            return dot_nn(jnp.concatenate(rows, axis=1), jnp.concatenate(cols, axis=0))

        def put_field(i, value, field=field):
            field[i] = value

        blocks(n, 8, couple, put_field)

    for copy in halo:
        copy.wait()
    for copy in near_loads:
        copy.wait()

    def load_leaf(leaf):
        return xs[:, pl.ds(pl.multiple_of(leaf * points, points), points)]

    def put_leaf(leaf, value):
        xl[leaf] = value

    blocks(every, 8, load_leaf, put_leaf)

    alive = near_live[0]

    def near_leaf(leaf):
        rows, cols = [], []
        for t in range(3):
            s = t * leaves + leaf
            place_of = jnp.where(s < alive, near_at[1, s] - (me * leaves - REACH), every)
            rows.append(xl[place_of])
            cols.append(vn[t, leaf])
        return dot_nt(jnp.concatenate(rows, axis=1), jnp.concatenate(cols, axis=1))

    def put_near(leaf, value):
        out[:, pl.ds(pl.multiple_of(leaf * points, points), points)] = value

    blocks(leaves, 8, near_leaf, put_near)

    for copy in leaf_copies:
        copy.wait()
    down = jnp.zeros((columns, rank), F32)
    for t in range(groups):
        far = jnp.where(jnp.abs(lf - t) >= 2, 1.0, 0.0).astype(F32)
        down = down + far * dot_nn(tc[t], matrix(ftop, t))
    nodes = 2
    while nodes <= members // 2:
        row = fold_row + members - 2 * nodes + sb * nodes // members
        down = dot_nt(down.astype(BF), matrix(ff, row))
        nodes *= 2
    down = dot_nt(down.astype(BF), wt[root])
    down_start = {depth: 0}
    position = 1
    for j in reversed(range(depth)):
        down_start[j] = position
        position += leaves >> j
    dn[0] = down.astype(BF)
    fields = (g0, g1, g2)
    for j in reversed(range(depth)):
        row = 2 * leaves - 2 * (leaves >> j)
        src_at, dst_at = down_start[j + 1], down_start[j]

        def descend(n, row=row, src_at=src_at, j=j):
            both = wt[pl.ds(row + 2 * n, 2)].reshape(2 * rank, rank)
            value = dot_nt(dn[src_at + n], both)
            value = (value[:, :rank], value[:, rank:])
            if j < COUPLED:
                value = (value[0] + fields[j][2 * n], value[1] + fields[j][2 * n + 1])
            return value

        def put_down(n, value, dst_at=dst_at):
            dn[dst_at + 2 * n] = value[0].astype(BF)
            dn[dst_at + 2 * n + 1] = value[1].astype(BF)

        blocks(leaves >> (j + 1), 8, descend, put_down)

    def final_body(q, carry):
        rows = jnp.concatenate([dn[down_start[0] + q * 8 + u] for u in range(8)], axis=0)
        natural = dot_nt(rows, small).astype(BF)
        for u in range(8):
            leaf = q * 8 + u
            at = pl.ds(pl.multiple_of(leaf * points, points), points)
            out[:, at] = out[:, at] + dot_nn(
                natural[u * columns : (u + 1) * columns], vb[leaf]
            )
        return carry

    lax.fori_loop(0, leaves // 8, final_body, 0)


def local(
    sources,
    leaf_basis,
    near_blocks,
    near_index,
    near_count,
    transfer,
    couple_first,
    couple_second,
    couple_third,
    index_first,
    index_second,
    index_third,
    couple_count,
    fold_transfer,
    top_couple,
):
    columns = sources.shape[0]
    leaves, rank, points = leaf_basis.shape
    groups = lax.axis_size("leaf")
    members = lax.axis_size("sub")

    near = near_blocks.reshape(3, leaves, points, points)
    top = top_couple.reshape(groups, rank * rank)
    trans = transfer.shape[0]
    half = rank // 2

    def flat(n):
        return pltpu.VMEM((n * half, 2 * rank), F32)

    scratch = [
        pltpu.VMEM((columns, (leaves + 2 * REACH) * points), BF),
        pltpu.VMEM((leaves + 2 * REACH + 1, columns, points), BF),
        pltpu.VMEM(leaf_basis.shape, BF),
        pltpu.VMEM(near.shape, BF),
        pltpu.VMEM(transfer.shape, BF),
        pltpu.VMEM(couple_first.shape, BF),
        pltpu.VMEM(couple_second.shape, BF),
        pltpu.VMEM(couple_third.shape, BF),
        pltpu.VMEM(fold_transfer.shape, BF),
        pltpu.VMEM(top.shape, BF),
        flat(trans),
        flat(couple_first.shape[0]),
        flat(couple_second.shape[0]),
        flat(couple_third.shape[0]),
        flat(fold_transfer.shape[0]),
        flat(groups),
        pltpu.VMEM((trans, rank, rank), BF),
    ]
    for j in range(COUPLED):
        scratch.append(pltpu.VMEM(((leaves >> j) + 2 * HALO + 1, columns, rank), BF))
    scratch.append(pltpu.VMEM(((leaves >> (COUPLED - 1)) - 1, columns, rank), BF))
    for j in range(COUPLED):
        scratch.append(pltpu.VMEM((leaves >> j, columns, rank), F32))
    scratch.append(pltpu.VMEM((2 * leaves - 1, columns, rank), BF))
    scratch.append(pltpu.VMEM((members, columns, rank), F32))
    scratch.append(pltpu.VMEM((groups, columns, rank), BF))
    for n in (8, CHUNKS, 2, 2, 6, 6, members - 1, members - 1, groups - 1, groups - 1):
        scratch.append(pltpu.SemaphoreType.DMA((n,)))

    anywhere = pl.BlockSpec(memory_space=pl.ANY)
    dims = (groups, members, leaves, columns, rank, points)
    return pl.pallas_call(
        functools.partial(kernel, dims),
        out_shape=jax.ShapeDtypeStruct((columns, leaves * points), F32),
        in_specs=[pl.BlockSpec(memory_space=pltpu.SMEM)] * 6 + [anywhere] * 9,
        out_specs=pl.BlockSpec(memory_space=pltpu.VMEM),
        scratch_shapes=scratch,
        compiler_params=pltpu.CompilerParams(
            collective_id=0, has_side_effects=True, vmem_limit_bytes=56 * 1024 * 1024
        ),
        cost_estimate=pl.CostEstimate(
            flops=600_000_000, bytes_accessed=13_000_000, transcendentals=0
        ),
        name="operator",
    )(
        near_index.T,
        index_first.T,
        index_second.T,
        index_third.T,
        near_count,
        couple_count,
        sources,
        leaf_basis,
        near,
        transfer,
        couple_first,
        couple_second,
        couple_third,
        fold_transfer,
        top,
    )


def solution(mesh):
    both = ("leaf", "sub")
    return jax.shard_map(
        local,
        mesh=mesh,
        in_specs=(
            P(None, both),
            P(both, None, None),
            P(both, None, None),
            P(both, None),
            P(both),
            P(both, None),
            P(both, None),
            P(both, None),
            P(both, None),
            P(both, None),
            P(both, None),
            P(both, None),
            P(both, None),
            P(),
            P("leaf", None, None),
        ),
        out_specs=P(None, both),
        check_vma=False,
    )
```

```python
import functools

import jax
import jax.numpy as jnp
from jax import lax
from jax.experimental import pallas as pl
from jax.experimental.pallas import tpu as pltpu
from jax.sharding import PartitionSpec as P

REACH = 16
COUPLED = 3
HALO = 3
CHUNKS = 4
MESH = pl.DeviceIdType.MESH
BF = jnp.bfloat16
F32 = jnp.float32


def dot_nn(a, b):
    return lax.dot_general(a, b, (((1,), (0,)), ((), ())), preferred_element_type=F32)


def dot_nt(a, b):
    return lax.dot_general(a, b, (((1,), (1,)), ((), ())), preferred_element_type=F32)


def spread(rank):
    row = lax.broadcasted_iota(jnp.int32, (2 * rank, 2 * rank), 0)
    col = lax.broadcasted_iota(jnp.int32, (2 * rank, 2 * rank), 1)
    inner = row % rank
    place = (row // rank) * rank + (inner % 2) * (rank // 2) + inner // 2
    return jnp.where(place == col, 1.0, 0.0).astype(BF)


def kernel(
    dims,
    near_at,
    first_at,
    second_at,
    third_at,
    near_live,
    couple_live,
    sources,
    basis,
    near,
    transfer,
    first,
    second,
    third,
    fold,
    top,
    out,
    xs,
    xl,
    vb,
    vn,
    vt,
    v1,
    v2,
    v3,
    vf,
    vtop,
    ft,
    f1,
    f2,
    f3,
    ff,
    ftop,
    wt,
    cp0,
    cp1,
    cp2,
    chi,
    g0,
    g1,
    g2,
    dn,
    terms,
    tc,
    load_sem,
    near_sem,
    halo_send,
    halo_recv,
    coef_send,
    coef_recv,
    sub_send,
    sub_recv,
    leaf_send,
    leaf_recv,
):
    groups, members, leaves, columns, rank, points = dims
    depth = leaves.bit_length() - 1
    lf = lax.axis_index("leaf")
    sb = lax.axis_index("sub")
    me = lf * members + sb
    count = groups * members
    right = lax.rem(me + 1, count)
    left = lax.rem(me + count - 1, count)
    right_id = (right // members, lax.rem(right, members))
    left_id = (left // members, lax.rem(left, members))
    half = rank // 2
    wide = REACH * points
    own = leaves * points

    loads = []
    pairs = (
        (sources, xs.at[:, pl.ds(wide, own)]),
        (basis, vb),
        (transfer, vt),
        (fold, vf),
        (top, vtop),
        (first, v1),
        (second, v2),
        (third, v3),
    )
    for i, (src, dst) in enumerate(pairs):
        copy = pltpu.make_async_copy(src, dst, load_sem.at[i])
        copy.start()
        loads.append(copy)
    part = leaves // CHUNKS
    near_loads = []
    for i in range(CHUNKS):
        copy = pltpu.make_async_copy(
            near.at[:, pl.ds(i * part, part)], vn.at[:, pl.ds(i * part, part)], near_sem.at[i]
        )
        copy.start()
        near_loads.append(copy)

    sub_ids = [(lf, lax.rem(sb + k, members)) for k in range(1, members)]
    leaf_ids = [(lax.rem(lf + k, groups), sb) for k in range(1, groups)]
    everyone = [left_id, right_id] + sub_ids + leaf_ids
    barrier = pltpu.get_barrier_semaphore()
    for target in everyone:
        pl.semaphore_signal(barrier, inc=1, device_id=target, device_id_type=MESH)

    perm = spread(rank)
    small = perm[:rank, :rank]

    def relay(src, dst):
        rows = src.shape[0]
        step = 16

        def body(q, carry):
            vals = []
            for u in range(step):
                p = q * step + u
                block = src[:, pl.ds(pl.multiple_of(p * 2 * rank, 2 * rank), 2 * rank)]
                vals.append(dot_nn(block, perm))
            for u in range(step):
                dst[pl.ds(q * step + u, rows, stride=half), :] = vals[u]
            return carry

        lax.fori_loop(0, half // step, body, 0)

    def matrix(ref, s):
        m = ref[pl.ds(pl.multiple_of(s * half, half), half), :].astype(BF)
        return jnp.concatenate([m[:, :rank], m[:, rank:]], axis=0)

    def blocks(n, width, compute, store):
        width = min(width, n)

        def body(q, carry):
            vals = [compute(q * width + u) for u in range(width)]
            for u in range(width):
                store(q * width + u, vals[u])
            return carry

        if n == width:
            body(0, 0)
        else:
            lax.fori_loop(0, n // width, body, 0)

    every = leaves + 2 * REACH
    xl[every] = jnp.zeros((columns, points), BF)
    coefs = (cp0, cp1, cp2)
    for j, ref in enumerate(coefs):
        ref[(leaves >> j) + 2 * HALO] = jnp.zeros((columns, rank), BF)

    loads[0].wait()
    loads[1].wait()

    def leaf_body(q, carry):
        vals = []
        for u in range(8):
            leaf = q * 8 + u
            x = xs[:, pl.ds(pl.multiple_of(wide + leaf * points, points), points)]
            vals.append(dot_nt(x, vb[leaf]).astype(BF))
        mixed = dot_nn(jnp.concatenate(vals, axis=0), small).astype(BF)
        for u in range(8):
            cp0[HALO + q * 8 + u] = mixed[u * columns : (u + 1) * columns]
        return carry

    lax.fori_loop(0, leaves // 8, leaf_body, 0)

    loads[2].wait()
    relay(vt, ft)

    def put_wt(s, value):
        wt[s] = value

    for start in range(2 * leaves - 1 - (2 * leaves - 1) % 8, 2 * leaves - 1):
        wt[start] = matrix(ft, start)
    blocks((2 * leaves - 1) // 8 * 8, 8, functools.partial(matrix, ft), put_wt)

    pl.semaphore_wait(barrier, len(everyone))
    halo = [
        pltpu.make_async_remote_copy(
            src_ref=sources.at[:, pl.ds(own - wide, wide)],
            dst_ref=xs.at[:, pl.ds(0, wide)],
            send_sem=halo_send.at[0],
            recv_sem=halo_recv.at[0],
            device_id=right_id,
            device_id_type=MESH,
        ),
        pltpu.make_async_remote_copy(
            src_ref=sources.at[:, pl.ds(0, wide)],
            dst_ref=xs.at[:, pl.ds(wide + own, wide)],
            send_sem=halo_send.at[1],
            recv_sem=halo_recv.at[1],
            device_id=left_id,
            device_id_type=MESH,
        ),
    ]
    for copy in halo:
        copy.start()

    high_start = {}
    position = 0
    for j in range(COUPLED, depth + 1):
        high_start[j] = position
        position += leaves >> j

    def place(j):
        return (coefs[j], HALO) if j < COUPLED else (chi, high_start[j])

    for j in range(depth):
        src, src_at = place(j)
        dst, dst_at = place(j + 1)
        row = 2 * leaves - 2 * (leaves >> j)

        def up(n, src=src, src_at=src_at, row=row):
            pair = jnp.concatenate([src[src_at + 2 * n], src[src_at + 2 * n + 1]], axis=1)
            both = wt[pl.ds(row + 2 * n, 2)].reshape(2 * rank, rank)
            return dot_nn(pair, both).astype(BF)

        def put(n, value, dst=dst, dst_at=dst_at):
            dst[dst_at + n] = value

        blocks(leaves >> (j + 1), 32, up, put)

    root = 2 * leaves - 2
    terms[sb] = dot_nn(chi[high_start[depth]], wt[root])
    sub_copies = [
        pltpu.make_async_remote_copy(
            src_ref=terms.at[sb],
            dst_ref=terms.at[sb],
            send_sem=sub_send.at[k],
            recv_sem=sub_recv.at[k],
            device_id=target,
            device_id_type=MESH,
        )
        for k, target in enumerate(sub_ids)
    ]
    for copy in sub_copies:
        copy.start()
    coef_copies = []
    for j, ref in enumerate(coefs):
        n = leaves >> j
        for side, (src_at, dst_at, target) in enumerate(
            ((n, 0, right_id), (HALO, n + HALO, left_id))
        ):
            copy = pltpu.make_async_remote_copy(
                src_ref=ref.at[pl.ds(src_at, HALO)],
                dst_ref=ref.at[pl.ds(dst_at, HALO)],
                send_sem=coef_send.at[2 * j + side],
                recv_sem=coef_recv.at[2 * j + side],
                device_id=target,
                device_id_type=MESH,
            )
            copy.start()
            coef_copies.append(copy)

    loads[3].wait()
    relay(vf, ff)
    loads[4].wait()
    relay(vtop, ftop)
    loads[5].wait()
    relay(v1, f1)
    loads[6].wait()
    relay(v2, f2)
    loads[7].wait()
    relay(v3, f3)

    for copy in sub_copies:
        copy.wait()
    fold_row = lf * (members - 2)
    current = [(terms[2 * n] + terms[2 * n + 1]).astype(BF) for n in range(members // 2)]
    offset = 0
    while len(current) > 1:
        products = [
            dot_nn(c, matrix(ff, fold_row + offset + n)) for n, c in enumerate(current)
        ]
        offset += len(current)
        current = [
            (products[2 * n] + products[2 * n + 1]).astype(BF)
            for n in range(len(products) // 2)
        ]
    tc[lf] = current[0]
    leaf_copies = [
        pltpu.make_async_remote_copy(
            src_ref=tc.at[lf],
            dst_ref=tc.at[lf],
            send_sem=leaf_send.at[k],
            recv_sem=leaf_recv.at[k],
            device_id=target,
            device_id_type=MESH,
        )
        for k, target in enumerate(leaf_ids)
    ]
    for copy in leaf_copies:
        copy.start()

    for copy in coef_copies:
        copy.wait()
    levels = ((f1, g0, first_at), (f2, g1, second_at), (f3, g2, third_at))
    for j, (mats, field, at) in enumerate(levels):
        n = leaves >> j
        ref = coefs[j]

        live = couple_live[0, j]

        def couple(i, n=n, ref=ref, mats=mats, at=at, live=live):
            rows, cols = [], []
            for t in range(3):
                s = t * n + i
                node = jnp.where(s < live, at[1, s] - (me * n - HALO), n + 2 * HALO)
                rows.append(ref[node])
                cols.append(matrix(mats, s))
            return dot_nn(jnp.concatenate(rows, axis=1), jnp.concatenate(cols, axis=0))

        def put_field(i, value, field=field):
            field[i] = value

        blocks(n, 32, couple, put_field)

    for copy in halo:
        copy.wait()
    for copy in near_loads:
        copy.wait()

    def load_leaf(leaf):
        return xs[:, pl.ds(pl.multiple_of(leaf * points, points), points)]

    def put_leaf(leaf, value):
        xl[leaf] = value

    blocks(every, 8, load_leaf, put_leaf)

    alive = near_live[0]

    def near_leaf(leaf):
        rows, cols = [], []
        for t in range(3):
            s = t * leaves + leaf
            place_of = jnp.where(s < alive, near_at[1, s] - (me * leaves - REACH), every)
            rows.append(xl[place_of])
            cols.append(vn[t, leaf])
        return dot_nt(jnp.concatenate(rows, axis=1), jnp.concatenate(cols, axis=1))

    def put_near(leaf, value):
        out[:, pl.ds(pl.multiple_of(leaf * points, points), points)] = value

    blocks(leaves, 32, near_leaf, put_near)

    for copy in leaf_copies:
        copy.wait()
    down = jnp.zeros((columns, rank), F32)
    for t in range(groups):
        far = jnp.where(jnp.abs(lf - t) >= 2, 1.0, 0.0).astype(F32)
        down = down + far * dot_nn(tc[t], matrix(ftop, t))
    nodes = 2
    while nodes <= members // 2:
        row = fold_row + members - 2 * nodes + sb * nodes // members
        down = dot_nt(down.astype(BF), matrix(ff, row))
        nodes *= 2
    down = dot_nt(down.astype(BF), wt[root])
    down_start = {depth: 0}
    position = 1
    for j in reversed(range(depth)):
        down_start[j] = position
        position += leaves >> j
    dn[0] = down.astype(BF)
    fields = (g0, g1, g2)
    for j in reversed(range(depth)):
        row = 2 * leaves - 2 * (leaves >> j)
        src_at, dst_at = down_start[j + 1], down_start[j]

        def descend(n, row=row, src_at=src_at, j=j):
            both = wt[pl.ds(row + 2 * n, 2)].reshape(2 * rank, rank)
            value = dot_nt(dn[src_at + n], both)
            value = (value[:, :rank], value[:, rank:])
            if j < COUPLED:
                value = (value[0] + fields[j][2 * n], value[1] + fields[j][2 * n + 1])
            return value

        def put_down(n, value, dst_at=dst_at):
            dn[dst_at + 2 * n] = value[0].astype(BF)
            dn[dst_at + 2 * n + 1] = value[1].astype(BF)

        blocks(leaves >> (j + 1), 32, descend, put_down)

    def final_body(q, carry):
        rows = jnp.concatenate([dn[down_start[0] + q * 16 + u] for u in range(16)], axis=0)
        natural = dot_nt(rows, small).astype(BF)
        for u in range(16):
            leaf = q * 16 + u
            at = pl.ds(pl.multiple_of(leaf * points, points), points)
            out[:, at] = out[:, at] + dot_nn(
                natural[u * columns : (u + 1) * columns], vb[leaf]
            )
        return carry

    lax.fori_loop(0, leaves // 16, final_body, 0)


def local(
    sources,
    leaf_basis,
    near_blocks,
    near_index,
    near_count,
    transfer,
    couple_first,
    couple_second,
    couple_third,
    index_first,
    index_second,
    index_third,
    couple_count,
    fold_transfer,
    top_couple,
):
    columns = sources.shape[0]
    leaves, rank, points = leaf_basis.shape
    groups = lax.axis_size("leaf")
    members = lax.axis_size("sub")

    near = near_blocks.reshape(3, leaves, points, points)
    top = top_couple.reshape(groups, rank * rank)
    trans = transfer.shape[0]
    half = rank // 2

    def flat(n):
        return pltpu.VMEM((n * half, 2 * rank), F32)

    scratch = [
        pltpu.VMEM((columns, (leaves + 2 * REACH) * points), BF),
        pltpu.VMEM((leaves + 2 * REACH + 1, columns, points), BF),
        pltpu.VMEM(leaf_basis.shape, BF),
        pltpu.VMEM(near.shape, BF),
        pltpu.VMEM(transfer.shape, BF),
        pltpu.VMEM(couple_first.shape, BF),
        pltpu.VMEM(couple_second.shape, BF),
        pltpu.VMEM(couple_third.shape, BF),
        pltpu.VMEM(fold_transfer.shape, BF),
        pltpu.VMEM(top.shape, BF),
        flat(trans),
        flat(couple_first.shape[0]),
        flat(couple_second.shape[0]),
        flat(couple_third.shape[0]),
        flat(fold_transfer.shape[0]),
        flat(groups),
        pltpu.VMEM((trans, rank, rank), BF),
    ]
    for j in range(COUPLED):
        scratch.append(pltpu.VMEM(((leaves >> j) + 2 * HALO + 1, columns, rank), BF))
    scratch.append(pltpu.VMEM(((leaves >> (COUPLED - 1)) - 1, columns, rank), BF))
    for j in range(COUPLED):
        scratch.append(pltpu.VMEM((leaves >> j, columns, rank), F32))
    scratch.append(pltpu.VMEM((2 * leaves - 1, columns, rank), BF))
    scratch.append(pltpu.VMEM((members, columns, rank), F32))
    scratch.append(pltpu.VMEM((groups, columns, rank), BF))
    for n in (8, CHUNKS, 2, 2, 6, 6, members - 1, members - 1, groups - 1, groups - 1):
        scratch.append(pltpu.SemaphoreType.DMA((n,)))

    anywhere = pl.BlockSpec(memory_space=pl.ANY)
    dims = (groups, members, leaves, columns, rank, points)
    return pl.pallas_call(
        functools.partial(kernel, dims),
        out_shape=jax.ShapeDtypeStruct((columns, leaves * points), F32),
        in_specs=[pl.BlockSpec(memory_space=pltpu.SMEM)] * 6 + [anywhere] * 9,
        out_specs=pl.BlockSpec(memory_space=pltpu.VMEM),
        scratch_shapes=scratch,
        compiler_params=pltpu.CompilerParams(
            collective_id=0, has_side_effects=True, vmem_limit_bytes=56 * 1024 * 1024
        ),
        cost_estimate=pl.CostEstimate(
            flops=600_000_000, bytes_accessed=13_000_000, transcendentals=0
        ),
        name="operator",
    )(
        near_index.T,
        index_first.T,
        index_second.T,
        index_third.T,
        near_count,
        couple_count,
        sources,
        leaf_basis,
        near,
        transfer,
        couple_first,
        couple_second,
        couple_third,
        fold_transfer,
        top,
    )


def solution(mesh):
    both = ("leaf", "sub")
    return jax.shard_map(
        local,
        mesh=mesh,
        in_specs=(
            P(None, both),
            P(both, None, None),
            P(both, None, None),
            P(both, None),
            P(both),
            P(both, None),
            P(both, None),
            P(both, None),
            P(both, None),
            P(both, None),
            P(both, None),
            P(both, None),
            P(both, None),
            P(),
            P("leaf", None, None),
        ),
        out_specs=P(None, both),
        check_vma=False,
    )
```
